1024 devices in a mesh: row: 16 (over z_hi, y), col: 64 (over x, z_lo, core).
Axes of the slice: x: 4, y: 8, z: 16 (z_hi: 2, z_lo: 8; z = z_hi * 8 + z_lo), core: 2. Of those that a mesh axis runs over, the one named last changes fastest.
Arguments:
- a_blocks: float32 [16, 192, 384, 128], P('row', 'col'), may hold values from -0.5 to 0.5
- a_rowid: int32 [16, 192, 3], P('row', 'col'), may hold values from 0 to 3
- a_count: int32 [16, 192], P('row', 'col'), may hold values from 0 to 3
- b_blocks: float32 [16, 192, 128, 384], P('row', 'col'), may hold values from -6 to 6
- b_colid: int32 [16, 192, 3], P('row', 'col'), may hold values from 0 to 5
- b_count: int32 [16, 192], P('row', 'col'), may hold values from 0 to 3
- dest_row: int32 [16, 1536, 1], P('row', 'col'), may hold values from 0 to 15; in each aligned block of 24 rows (0 to 23, 24 to 47, ..., all dimensions but the last counted through in order) at most 2 rows name the same one
Outputs:
- owned_blocks: float32 [16, 2048, 128, 128], P('row', 'col')
The draws below stay inside these ranges and needn't reach their ends.
Inputs may be any that keep to these rules, and one draw needn't show every extreme that they name: `dest_row`: among the 24 product blocks of one device, at most 2 name any one owner row, and some device's blocks name one owner row exactly 2 times.
All inputs are finite; a program needn't handle non-finite values.
Results may differ from the reference program's by a relative error of at most 0.0003.
Values sent between devices are 32-bit elements; how exact they have to be, the bound alone decides.
A program may use at most 64 MiB of HBM per device.

```python
import math
import jax
import jax.numpy as jnp
import numpy as np
from jax import lax

BS = 128
SLOTS = 3
RB = 4
CB = 6
KB = 3
CAPP = 2
N_ROW = 16
N_COL = 64


def with_ends(values, key, smallest, top_value):
    longest = values.shape.index(max(values.shape))
    spots = []
    for shift in (0, 1):
        where = [jax.random.randint(jax.random.fold_in(key, axis), (), 0, length) for axis, length in enumerate(values.shape)]
        where[longest] = (where[longest] + shift) % values.shape[longest]
        spots.append(tuple(where))
    return values.at[spots[0]].set(smallest).at[spots[1]].set(top_value)


def level_of(own_key, shape, split, low, top_value):
    level, own = 1.0, jax.random.fold_in(own_key, 6)
    for position, blocks in split:
        draws = jnp.exp(jax.random.uniform(jax.random.fold_in(own, position), (blocks,), jnp.float32, low / len(split), top_value / len(split)))
        level = level * jnp.repeat(draws, shape[position] // blocks).reshape([-1 if axis == position else 1 for axis in range(len(shape))])
    return level


def assign_block(rng, own, number, rows, count, top, most, lean):
    ranking = jax.random.permutation(rng, count)
    heavy_load, usual = shares(count, rows * top, most, lean, True), shares(count, rows * top, most, lean, False)
    places = jnp.arange(count)

    def named(lengths, rotation):
        used = int((lengths > 0).sum())
        fixed = max(1, used // 4)
        passed = fixed + (places - fixed + rotation * (used - fixed)) % max(1, count - fixed)
        return jnp.zeros((count,), jnp.int32).at[ranking[jnp.where(places < fixed, places, passed)]].set(jnp.asarray(lengths, jnp.int32))

    lengths = jnp.where(number % 4 == 0, named(heavy_load, number // 4), named(usual, number - number // 4 - 1))
    mixed = jax.random.permutation(jax.random.fold_in(own, 3), count)
    giver, taker = mixed[0:count // 2 * 2:2], mixed[1:count // 2 * 2:2]
    margin = jnp.minimum(lengths[giver] - 1, most - lengths[taker]) // 2
    margin = jnp.where((giver == ranking[0]) | (taker == ranking[0]) | (lengths[taker] == 0), 0, jnp.maximum(margin, 0))
    passed = jax.random.randint(jax.random.fold_in(own, 4), (count // 2,), 0, 1 << 20) % (margin + 1)
    lengths = lengths.at[giver].add(-passed).at[taker].add(passed)
    labels = jnp.searchsorted(jnp.cumsum(lengths), jnp.arange(rows * top), side="right").astype(jnp.int32)
    table = labels.reshape(top, rows).T
    table = table[jax.random.permutation(jax.random.fold_in(own, 1), rows)]
    rotation = jax.random.randint(jax.random.fold_in(own, 2), (rows, 1), 0, top)
    return jnp.take_along_axis(table, (jnp.arange(top)[None, :] + rotation) % top, axis=1)


def shares(amount, total, most, slope, full):
    weights = [(1 << 20) // math.isqrt(grade ** slope) + 1 for grade in range(1, amount + 1)]
    largest = most if full else min(most, max(-(-total // amount), total * weights[0] // sum(weights)))
    least = 1 if total - largest >= amount - 1 else 0
    counts, rest = [largest] + [least] * (amount - 1), total - largest - least * (amount - 1)
    while rest > 0:
        movable = [i for i in range(1, amount) if counts[i] < largest] or [i for i in range(1, amount) if counts[i] < most]
        pool, left = sum([weights[i] for i in movable]), rest
        for i in movable:
            more = min(most - counts[i], max(1, left * weights[i] // pool), rest)
            counts[i] = counts[i] + more
            rest = rest - more
    return np.array(counts)


def normal_values(rng, dims, spread, reach, cuts=(), kind=jnp.bfloat16):
    factor_of = level_of(rng, dims, cuts, -0.22, 0.18) if cuts else 1.0
    result = jax.random.normal(rng, dims, jnp.float32) * spread * factor_of
    return jnp.minimum(jnp.maximum(result, -reach), reach).astype(kind)


def setup_inputs(seed: int = 0) -> dict:
    streams_of = jax.random.split(jax.random.key(seed), 8)
    a_blocks = normal_values(streams_of[0], (N_ROW, N_COL * KB, SLOTS * BS, BS), BS ** -0.5, 0.5, ((0, 16), (1, 64)), jnp.float32)
    a_rowid = with_ends(jax.random.randint(streams_of[1], (N_ROW, N_COL * KB, SLOTS), 0, RB), jax.random.fold_in(streams_of[1], 1), 0, RB - 1).astype(jnp.int32)
    a_count = with_ends(jax.random.randint(streams_of[2], (N_ROW, N_COL * KB), 0, SLOTS + 1), jax.random.fold_in(streams_of[2], 1), 0, SLOTS).astype(jnp.int32)
    b_blocks = normal_values(streams_of[3], (N_ROW, N_COL * KB, BS, SLOTS * BS), 1.0, 6.0, ((0, 16), (1, 64)), jnp.float32)
    b_colid = with_ends(jax.random.randint(streams_of[4], (N_ROW, N_COL * KB, SLOTS), 0, CB), jax.random.fold_in(streams_of[4], 1), 0, CB - 1).astype(jnp.int32)
    b_count = with_ends(jax.random.randint(streams_of[5], (N_ROW, N_COL * KB), 0, SLOTS + 1), jax.random.fold_in(streams_of[5], 1), 0, SLOTS).astype(jnp.int32)
    dest_row_keys = jax.random.split(jax.random.fold_in(streams_of[6], 1), N_ROW * (N_COL * RB * CB) // (RB * CB))
    dest_row_turns = jax.random.permutation(jax.random.fold_in(streams_of[6], 3), N_ROW * (N_COL * RB * CB) // (RB * CB))
    dest_row = jax.vmap(lambda own, number: assign_block(jax.random.fold_in(streams_of[6], 2), own, number, RB * CB, N_ROW, 1, CAPP, 2))(dest_row_keys, dest_row_turns).reshape((N_ROW, N_COL * RB * CB, 1))
    return {"a_blocks": a_blocks, "a_rowid": a_rowid, "a_count": a_count, "b_blocks": b_blocks, "b_colid": b_colid, "b_count": b_count, "dest_row": dest_row}


def panel_product(a_panel, a_rows, a_used, b_panel, b_cols, b_used):
    block_edge = a_panel.shape[-1]
    slot_count = a_rows.shape[-1]
    inner_count = a_rows.shape[0]
    slot_iota = jnp.arange(slot_count, dtype=jnp.int32)
    a_live = slot_iota[None, :] < a_used[:, None]
    b_live = slot_iota[None, :] < b_used[:, None]
    row_hot = ((a_rows[:, :, None] == jnp.arange(RB, dtype=jnp.int32)[None, None, :]) & a_live[:, :, None]).astype(jnp.float32)
    col_hot = ((b_cols[:, :, None] == jnp.arange(CB, dtype=jnp.int32)[None, None, :]) & b_live[:, :, None]).astype(jnp.float32)
    slot_prod = jnp.einsum("kxb,kby->kxy", a_panel, b_panel, precision=lax.Precision.HIGHEST)
    slot_prod = slot_prod.reshape(inner_count, slot_count, block_edge, slot_count, block_edge)
    pair_hot = jnp.einsum("kti,kuj->ktiuj", row_hot, col_hot)
    return jnp.einsum("ktiuj,ktpuq->ipjq", pair_hot, slot_prod, precision=lax.Precision.HIGHEST)


def reference(a_blocks, a_rowid, a_count, b_blocks, b_colid, b_count, dest_row):
    block_total = RB * CB
    a_grid = a_blocks.reshape(N_ROW, N_COL, KB, SLOTS * BS, BS)
    a_rowgrid = a_rowid.reshape(N_ROW, N_COL, KB, SLOTS)
    a_usegrid = a_count.reshape(N_ROW, N_COL, KB)
    b_grid = b_blocks.reshape(N_ROW, N_COL, KB, BS, SLOTS * BS)
    b_colgrid = b_colid.reshape(N_ROW, N_COL, KB, SLOTS)
    b_usegrid = b_count.reshape(N_ROW, N_COL, KB)

    def one_device(flat_index):
        grid_row = flat_index // N_COL
        grid_col = flat_index % N_COL
        running = jnp.zeros((RB, BS, CB, BS), jnp.float32)
        for stride in range(3):
            source_col = (grid_col + stride) % N_COL
            source_row = (grid_row + stride) % N_ROW
            running = running + panel_product(
                a_grid[grid_row, source_col], a_rowgrid[grid_row, source_col], a_usegrid[grid_row, source_col],
                b_grid[source_row, grid_col], b_colgrid[source_row, grid_col], b_usegrid[source_row, grid_col])
        return running.transpose(0, 2, 1, 3).reshape(block_total, BS, BS)

    products = lax.map(one_device, jnp.arange(N_ROW * N_COL, dtype=jnp.int32))
    products = products.reshape(N_ROW, N_COL, block_total, BS, BS)
    targets = dest_row.reshape(N_ROW, N_COL, block_total)
    block_iota = jnp.arange(block_total, dtype=jnp.int32)
    earlier = (targets[:, :, :, None] == targets[:, :, None, :]) & (block_iota[None, None, None, :] < block_iota[None, None, :, None])
    slot_rank = jnp.sum(earlier.astype(jnp.int32), axis=3)
    source_rows = jnp.broadcast_to(jnp.arange(N_ROW, dtype=jnp.int32)[:, None, None], targets.shape)
    column_ids = jnp.broadcast_to(jnp.arange(N_COL, dtype=jnp.int32)[None, :, None], targets.shape)
    places = source_rows * CAPP + slot_rank
    owned_blocks = jnp.zeros((N_ROW, N_COL, N_ROW * CAPP, BS, BS), jnp.float32)
    owned_blocks = owned_blocks.at[targets, column_ids, places].set(products)
    return owned_blocks.reshape(N_ROW, N_COL * N_ROW * CAPP, BS, BS)
```

```python
import jax
import jax.numpy as jnp
from jax import lax
from jax.experimental import pallas as pl
from jax.experimental.pallas import tpu as pltpu
from jax.sharding import PartitionSpec as P

MESH = pl.DeviceIdType.MESH
BS = 128
SLOTS = 3
RB = 4
CB = 6
KB = 3
CAPP = 2
HALVES = 2
SIDE = 8
BLOCKS = RB * CB
CARRIERS = {0: (7, 6), 1: (4, 2)}
LANDING = {0: (0, 0), 6: (0, 2), 1: (1, 0), 4: (1, 1), 2: (1, 2)}


def kernel(a_ref, b_ref, am_ref, bm_ref, tbl_ref, out_ref,
           a_got, b_got, am_got, bm_got, carry, crossed, crossed_m,
           pah, pal, pbh, pbl, prod, stage, relay,
           a_s, a_r, b_s, b_r, c_s, c_r, x_s, x_r, f_s,
           z_s, z_r, o_s, o_r, w_s, w_r, l_s):
    row = lax.axis_index("row")
    col = lax.axis_index("col")
    n_col = lax.axis_size("col")
    half = row // SIDE
    y = lax.rem(row, SIDE)
    left = (row, lax.rem(col + n_col - 1, n_col))
    right = (row, lax.rem(col + 1, n_col))
    other = 1 - half
    across = (other * SIDE + y, col)

    def at_y(yy):
        return (half * SIDE + yy, col)

    def turned(d):
        return lax.rem(y + d, SIDE)

    def send(src, dst, ss, rs, to):
        return pltpu.make_async_remote_copy(
            src_ref=src, dst_ref=dst, send_sem=ss, recv_sem=rs, device_id=to, device_id_type=MESH)

    barrier = pltpu.get_barrier_semaphore()
    peers = [left, right, across] + [at_y(turned(d)) for d in range(1, SIDE)]
    for peer in peers:
        pl.semaphore_signal(barrier, inc=1, device_id=peer, device_id_type=MESH)
    pl.semaphore_wait(barrier, len(peers))

    def a_copy(step, k):
        if k == KB:
            src = am_ref if step == 0 else am_got.at[0]
            return send(src, am_got.at[step], a_s.at[step, k], a_r.at[step, k], left)
        src = a_ref.at[k] if step == 0 else a_got.at[0, k]
        return send(src, a_got.at[step, k], a_s.at[step, k], a_r.at[step, k], left)

    up = at_y(lax.rem(y + SIDE - 1, SIDE))

    def b_copy(step, k):
        if k == KB:
            src = bm_ref if step == 0 else bm_got.at[0]
            return send(src, bm_got.at[step], b_s.at[step, k], b_r.at[step, k], up)
        src = b_ref.at[k] if step == 0 else b_got.at[0, k]
        return send(src, b_got.at[step, k], b_s.at[step, k], b_r.at[step, k], up)

    def carry_copy(n, to):
        return send(b_ref.at[1 + n], carry, c_s.at[n], c_r.at[0], at_y(to))

    def cross_copy(src):
        return send(src, crossed, x_s.at[0], x_r.at[0], across)

    def cross_meta():
        return send(bm_ref, crossed_m, x_s.at[1], x_r.at[1], across)

    def cross_last():
        return send(carry, b_got.at[0, 1], x_s.at[0], b_r.at[0, 1], across)

    def land_copy(yy):
        panel, third = LANDING[yy]
        return send(crossed, b_got.at[panel, third], f_s.at[0], b_r.at[panel, third], at_y(SIDE - 1))

    def land_meta(yy):
        panel = LANDING[yy][0]
        return send(crossed_m, bm_got.at[panel], f_s.at[1], b_r.at[panel, KB], at_y(SIDE - 1))

    for yy, targets in CARRIERS.items():
        @pl.when(y == yy)
        def _():
            for n, to in enumerate(targets):
                carry_copy(n, to).start()
            cross_meta().start()
            cross_copy(b_ref.at[0]).start()

    @pl.when(y > 0)
    def _():
        for k in (KB, 0, 1, 2):
            b_copy(0, k).start()

    for k in (KB, 0, 1, 2):
        a_copy(0, k).start()

    def build_a(src, meta, k):
        @pl.loop(0, RB)
        def _(i):
            total = jnp.zeros((BS, BS), jnp.float32)
            for t in range(SLOTS):
                total += jnp.where(meta[pl.ds(k * SLOTS + t, 1), :] == i, src[pl.ds(t * BS, BS), :], 0.0)
            high = total.astype(jnp.bfloat16)
            rows = pl.ds(pl.multiple_of(i * BS, BS), BS)
            pah[rows, pl.ds(k * BS, BS)] = high
            pal[rows, pl.ds(k * BS, BS)] = (total - high.astype(jnp.float32)).astype(jnp.bfloat16)

    def build_b(src, meta, k):
        @pl.loop(0, CB)
        def _(j):
            total = jnp.zeros((BS, BS), jnp.float32)
            for t in range(SLOTS):
                total += jnp.where(meta[pl.ds(k * SLOTS + t, 1), :] == j, src[:, pl.ds(t * BS, BS)], 0.0)
            high = total.astype(jnp.bfloat16)
            cols = pl.ds(pl.multiple_of(j * BS, BS), BS)
            pbh[pl.ds(k * BS, BS), cols] = high
            pbl[pl.ds(k * BS, BS), cols] = (total - high.astype(jnp.float32)).astype(jnp.bfloat16)

    def multiply(first):
        @pl.loop(0, CB // 2)
        def _(pair):
            cols = pl.ds(pl.multiple_of(pair * 2 * BS, 2 * BS), 2 * BS)
            bh = pbh[:, cols]
            bl = pbl[:, cols]
            for i in range(RB // 2):
                ah = pah[pl.ds(i * 2 * BS, 2 * BS), :]
                al = pal[pl.ds(i * 2 * BS, 2 * BS), :]
                part = (jnp.dot(ah, bl, preferred_element_type=jnp.float32)
                        + jnp.dot(al, bh, preferred_element_type=jnp.float32)
                        + jnp.dot(ah, bh, preferred_element_type=jnp.float32))
                for p in range(2):
                    for q in range(2):
                        block = (i * 2 + p) * CB + pair * 2 + q
                        piece = part[p * BS:(p + 1) * BS, q * BS:(q + 1) * BS]
                        prod[block] = piece if first else prod[block] + piece

    for k in range(KB):
        build_a(a_ref.at[k], am_ref, k)
        build_b(b_ref.at[k], bm_ref, k)
    multiply(True)
    prod[BLOCKS] = jnp.zeros((BS, BS), jnp.float32)

    carriers = [to for targets in CARRIERS.values() for to in targets]
    for yy in carriers:
        @pl.when(y == yy)
        def _():
            carry_copy(0, yy).wait_recv()
            if yy == SIDE - 1:
                cross_last().start()
            else:
                cross_copy(carry).start()

    for k in (KB, 0, 1, 2):
        a_copy(0, k).wait_recv()
        a_copy(1, k).start()
    for k in (KB, 0, 1, 2):
        b_copy(0, k).wait_recv()

        @pl.when(y > 0)
        def _():
            b_copy(1, k).start()
        if k < KB:
            build_a(a_got.at[0, k], am_got.at[0], k)
            build_b(b_got.at[0, k], bm_got.at[0], k)
    multiply(False)

    for yy in LANDING:
        @pl.when(y == yy)
        def _():
            if yy in CARRIERS:
                cross_meta().wait_recv()
                land_meta(yy).start()
            cross_copy(b_ref.at[0]).wait_recv()
            land_copy(yy).start()

    for k in (KB, 0, 1, 2):
        a_copy(1, k).wait_recv()
        b_copy(1, k).wait_recv()
        if k < KB:
            build_a(a_got.at[1, k], am_got.at[1], k)
            build_b(b_got.at[1, k], bm_got.at[1], k)
    multiply(False)

    def fill(slot, owner):
        for rank in range(CAPP):
            stage[slot * CAPP + rank] = prod[tbl_ref[owner * CAPP + rank]]

    def pair_at(ref, place):
        return ref.at[pl.ds(place * CAPP, CAPP)]

    def z_copy(d):
        dst = pair_at(out_ref, row) if d == 0 else pair_at(relay, d - 1)
        return send(pair_at(stage, SIDE + d), dst, z_s.at[d], z_r.at[d], across)

    def own_copy(d):
        return send(pair_at(stage, d), pair_at(out_ref, row), o_s.at[d], o_r.at[d], at_y(turned(d)))

    def onward_copy(d):
        return send(pair_at(relay, d - 1), pair_at(out_ref, other * SIDE + y),
                    w_s.at[d], w_r.at[d], at_y(turned(d)))

    for d in (1, 2, 3, 4, 5, 6, 7, 0):
        fill(SIDE + d, other * SIDE + turned(d))
        z_copy(d).start()
        fill(d, half * SIDE + turned(d))
        if d:
            own_copy(d).start()
    kept = pltpu.make_async_copy(pair_at(stage, 0), pair_at(out_ref, row), l_s.at[0])
    kept.start()
    for d in range(1, SIDE):
        z_copy(d).wait_recv()
        onward_copy(d).start()

    for step in range(2):
        for k in range(KB + 1):
            a_copy(step, k).wait_send()

            @pl.when(y > 0)
            def _():
                b_copy(step, k).wait_send()
    for yy, targets in CARRIERS.items():
        @pl.when(y == yy)
        def _():
            for n, to in enumerate(targets):
                carry_copy(n, to).wait_send()
            cross_meta().wait_send()
            cross_copy(b_ref.at[0]).wait_send()
    for yy in carriers:
        @pl.when(y == yy)
        def _():
            cross_copy(carry).wait_send()
    for yy in LANDING:
        @pl.when(y == yy)
        def _():
            if yy in CARRIERS:
                land_meta(yy).wait_send()
            land_copy(yy).wait_send()
    kept.wait()
    for d in range(1, SIDE):
        own_copy(d).wait()
    z_copy(0).wait()
    for d in range(1, SIDE):
        z_copy(d).wait_send()
        onward_copy(d).wait()


def per_device(a_blocks, a_rowid, a_count, b_blocks, b_colid, b_count, dest_row):
    slot = jnp.arange(SLOTS, dtype=jnp.int32)

    def marks(ids, used):
        live = jnp.where(slot[None, :] < used[:, None], ids, -1).reshape(-1, 1)
        return jnp.broadcast_to(jnp.pad(live, ((0, 16 - KB * SLOTS), (0, 0))), (16, BS))

    n_row = lax.axis_size("row")
    targets = dest_row[0, :, 0]
    order = jnp.arange(BLOCKS, dtype=jnp.int32)
    earlier = (targets[:, None] == targets[None, :]) & (order[None, :] < order[:, None])
    rank = jnp.sum(earlier.astype(jnp.int32), axis=1)
    place = targets * CAPP + rank
    picked = place[None, :] == jnp.arange(n_row * CAPP, dtype=jnp.int32)[:, None]
    table = BLOCKS + jnp.sum(jnp.where(picked, order[None, :] - BLOCKS, 0), axis=1)

    vmem = pl.BlockSpec(memory_space=pltpu.VMEM)
    f32, bf16 = jnp.float32, jnp.bfloat16
    dma = pltpu.SemaphoreType.DMA
    out = pl.pallas_call(
        kernel,
        out_shape=jax.ShapeDtypeStruct((n_row * CAPP, BS, BS), f32),
        in_specs=[vmem, vmem, vmem, vmem, pl.BlockSpec(memory_space=pltpu.SMEM)],
        out_specs=pl.BlockSpec(memory_space=pl.ANY),
        scratch_shapes=[
            pltpu.VMEM((2, KB, SLOTS * BS, BS), f32),
            pltpu.VMEM((2, KB, BS, SLOTS * BS), f32),
            pltpu.VMEM((2, 16, BS), jnp.int32),
            pltpu.VMEM((2, 16, BS), jnp.int32),
            pltpu.VMEM((BS, SLOTS * BS), f32),
            pltpu.VMEM((BS, SLOTS * BS), f32),
            pltpu.VMEM((16, BS), jnp.int32),
            pltpu.VMEM((RB * BS, KB * BS), bf16),
            pltpu.VMEM((RB * BS, KB * BS), bf16),
            pltpu.VMEM((KB * BS, CB * BS), bf16),
            pltpu.VMEM((KB * BS, CB * BS), bf16),
            pltpu.VMEM((BLOCKS + 1, BS, BS), f32),
            pltpu.VMEM((HALVES * SIDE * CAPP, BS, BS), f32),
            pltpu.VMEM(((SIDE - 1) * CAPP, BS, BS), f32),
            dma((2, KB + 1)), dma((2, KB + 1)), dma((2, KB + 1)), dma((2, KB + 1)),
            dma((2,)), dma((1,)), dma((2,)), dma((2,)), dma((2,)),
            dma((SIDE,)), dma((SIDE,)), dma((SIDE,)), dma((SIDE,)),
            dma((SIDE,)), dma((SIDE,)), dma((1,)),
        ],
        compiler_params=pltpu.CompilerParams(
            collective_id=0, has_side_effects=True, vmem_limit_bytes=48 * 2**20),
        cost_estimate=pl.CostEstimate(flops=2 * 3 * 3 * 512 * 384 * 768, bytes_accessed=4 * 2**20, transcendentals=0),
        name="panels",
    )(a_blocks[0], b_blocks[0], marks(a_rowid[0], a_count[0]), marks(b_colid[0], b_count[0]), table)
    return out[None]


def solution(mesh):
    placed = (
        P("row", "col", None, None),
        P("row", "col", None),
        P("row", "col"),
        P("row", "col", None, None),
        P("row", "col", None),
        P("row", "col"),
        P("row", "col", None),
    )
    return jax.shard_map(
        per_device,
        mesh=mesh,
        in_specs=placed,
        out_specs=P("row", "col", None, None),
        check_vma=False,
    )
```

```python
import jax
import jax.numpy as jnp
from jax import lax
from jax.experimental import pallas as pl
from jax.experimental.pallas import tpu as pltpu
from jax.sharding import PartitionSpec as P

MESH = pl.DeviceIdType.MESH
BS = 128
SLOTS = 3
RB = 4
CB = 6
KB = 3
CAPP = 2
LAG = 5
CHANGE = 5
WINDOW = 4
HALVES = 2
SIDE = 8
BLOCKS = RB * CB
PARTS = 4
PART = KB * BS // PARTS


def kernel(a_ref, a_id, a_used, b_ref, b_id, b_used, dest_ref, out_ref,
           am_ref, bm_ref, tbl_ref,
           a_got, b_got, am_got, bm_got, carry, crossed, crossed_m,
           pah, pal, pbh, pbl, prod, stage, relay,
           a_s, a_r, b_s, b_r, c_s, c_r, x_s, x_r, f_s,
           z_s, z_r, o_s, o_r, w_s, w_r, l_s, turn):
    row = lax.axis_index("row")
    col = lax.axis_index("col")
    n_col = lax.axis_size("col")
    half = row // SIDE
    y = lax.rem(row, SIDE)
    left = (row, lax.rem(col + n_col - 1, n_col))
    right = (row, lax.rem(col + 1, n_col))
    other = 1 - half
    across = (other * SIDE + y, col)
    inner = lax.rem(col // 2, SIDE)
    early = inner < SIDE // 2
    nearest = jnp.where(early, SIDE // 2, 2 * SIDE) - inner // 2 * 2

    def along_z(step):
        to = lax.rem(half * SIDE + inner + step, HALVES * SIDE)
        return (to // SIDE * SIDE + y, col + (lax.rem(to, SIDE) - inner) * 2)

    other_shift = [along_z(nearest + step) for step in (0, 2, SIDE, SIDE + 2)]

    first = (y == 0) | (y > PARTS)
    panel = jnp.where(first, 0, 1)
    part = jnp.where(first, lax.rem(SIDE - y, SIDE), y - 1)
    last = SIDE - 1

    def at_y(yy):
        return (half * SIDE + yy, col)

    def turned(d):
        return lax.rem(y + d, SIDE)

    def send(src, dst, ss, rs, to):
        return pltpu.make_async_remote_copy(
            src_ref=src, dst_ref=dst, send_sem=ss, recv_sem=rs, device_id=to, device_id_type=MESH)

    barrier = pltpu.get_barrier_semaphore()
    peers = [left, right, across] + other_shift + [at_y(turned(d)) for d in range(1, SIDE)]
    for peer in peers:
        pl.semaphore_signal(barrier, inc=1, device_id=peer, device_id_type=MESH)
    pl.semaphore_wait(barrier, len(peers))

    for k in range(KB):
        for t in range(SLOTS):
            a_mark = jnp.where(t < a_used[0, k], a_id[0, k, t], -1)
            b_mark = jnp.where(t < b_used[0, k], b_id[0, k, t], -1)
            am_ref[pl.ds(k * SLOTS + t, 1), :] = jnp.full((1, BS), a_mark, jnp.int32)
            bm_ref[pl.ds(k * SLOTS + t, 1), :] = jnp.full((1, BS), b_mark, jnp.int32)

    def a_copy(step, k):
        if k == KB:
            src = am_ref if step == 0 else am_got.at[0]
            return send(src, am_got.at[step], a_s.at[step, k], a_r.at[step, k], left)
        src = a_ref.at[k] if step == 0 else a_got.at[0, k]
        return send(src, a_got.at[step, k], a_s.at[step, k], a_r.at[step, k], left)

    up = at_y(lax.rem(y + SIDE - 1, SIDE))

    def rows_of(ref, n):
        return ref.at[pl.ds(pl.multiple_of(n * PART, PART), PART)]

    def b_copy(step, n):
        if n == PARTS:
            src = bm_ref if step == 0 else bm_got.at[0]
            return send(src, bm_got.at[step], b_s.at[step, n], b_r.at[step, n], up)
        src = b_ref if step == 0 else b_got.at[0]
        return send(rows_of(src, n), rows_of(b_got.at[step], n), b_s.at[step, n], b_r.at[step, n], up)

    def carry_copy(n):
        to = jnp.where(y == 0, SIDE - n, n + 1)
        return send(rows_of(b_ref, n), carry, c_s.at[n], c_r.at[0], at_y(to))

    def cross_copy(src):
        return send(src, crossed, x_s.at[0], x_r.at[0], across)

    def cross_last():
        return send(carry, rows_of(b_got.at[0], 1), x_s.at[0], b_r.at[0, 1], across)

    def cross_meta():
        return send(bm_ref, crossed_m, x_s.at[1], x_r.at[1], across)

    def land_copy():
        return send(crossed, rows_of(b_got.at[panel], part), f_s.at[0], b_r.at[panel, part], at_y(last))

    def land_meta():
        return send(crossed_m, bm_got.at[panel], f_s.at[1], b_r.at[panel, PARTS], at_y(last))

    @pl.when(y < 2)
    def _():
        cross_copy(rows_of(b_ref, 0)).start()
        cross_meta().start()
        for n in range(1, PARTS):
            carry_copy(n).start()

    @pl.when(y > 0)
    def _():
        for n in (PARTS, 0, 1, 2, 3):
            b_copy(0, n).start()

    for k in (KB, 0, 1, 2):
        a_copy(0, k).start()

    def build_a(src, meta, k):
        @pl.loop(0, RB)
        def _(i):
            total = jnp.zeros((BS, BS), jnp.float32)
            for t in range(SLOTS):
                total += jnp.where(meta[pl.ds(k * SLOTS + t, 1), :] == i, src[pl.ds(t * BS, BS), :], 0.0)
            high = total.astype(jnp.bfloat16)
            rows = pl.ds(pl.multiple_of(i * BS, BS), BS)
            pah[rows, pl.ds(k * BS, BS)] = high
            pal[rows, pl.ds(k * BS, BS)] = (total - high.astype(jnp.float32)).astype(jnp.bfloat16)

    def build_b(src, meta, k):
        @pl.loop(0, CB)
        def _(j):
            total = jnp.zeros((BS, BS), jnp.float32)
            for t in range(SLOTS):
                total += jnp.where(meta[pl.ds(k * SLOTS + t, 1), :] == j, src[pl.ds(k * BS, BS), pl.ds(t * BS, BS)], 0.0)
            high = total.astype(jnp.bfloat16)
            cols = pl.ds(pl.multiple_of(j * BS, BS), BS)
            pbh[pl.ds(k * BS, BS), cols] = high
            pbl[pl.ds(k * BS, BS), cols] = (total - high.astype(jnp.float32)).astype(jnp.bfloat16)

    def multiply(first):
        @pl.loop(0, CB // 2)
        def _(pair):
            cols = pl.ds(pl.multiple_of(pair * 2 * BS, 2 * BS), 2 * BS)
            bh = pbh[:, cols]
            bl = pbl[:, cols]
            for i in range(RB // 2):
                ah = pah[pl.ds(i * 2 * BS, 2 * BS), :]
                al = pal[pl.ds(i * 2 * BS, 2 * BS), :]
                part = (jnp.dot(ah, bl, preferred_element_type=jnp.float32)
                        + jnp.dot(al, bh, preferred_element_type=jnp.float32)
                        + jnp.dot(ah, bh, preferred_element_type=jnp.float32))
                for p in range(2):
                    for q in range(2):
                        block = (i * 2 + p) * CB + pair * 2 + q
                        piece = part[p * BS:(p + 1) * BS, q * BS:(q + 1) * BS]
                        prod[block] = piece if first else prod[block] + piece

    @pl.loop(0, HALVES * SIDE)
    def _(owner):
        first, second = BLOCKS, BLOCKS
        for m in range(BLOCKS - 1, -1, -1):
            hit = dest_ref[0, m, 0] == owner
            second = jnp.where(hit, first, second)
            first = jnp.where(hit, m, first)
        tbl_ref[owner * CAPP] = first
        tbl_ref[owner * CAPP + 1] = second

    for k in range(KB):
        build_a(a_ref.at[k], am_ref, k)
        build_b(b_ref, bm_ref, k)
    multiply(True)
    prod[BLOCKS] = jnp.zeros((BS, BS), jnp.float32)

    @pl.when((y > 1) & (y < last))
    def _():
        carry_copy(1).wait_recv()
        cross_copy(carry).start()

    @pl.when(y == last)
    def _():
        carry_copy(1).wait_recv()
        cross_last().start()

    def b_onward():
        for n in (PARTS, 0, 1, 2, 3):
            b_copy(0, n).wait_recv()

            @pl.when(y > 0)
            def _():
                b_copy(1, n).start()

    pl.when(y < last)(b_onward)
    for k in (KB, 0, 1, 2):
        a_copy(0, k).wait_recv()

    @pl.when(y < 2)
    def _():
        cross_meta().wait_recv()
        land_meta().start()

    @pl.when(y < last)
    def _():
        cross_copy(carry).wait_recv()
        land_copy().start()

    cross_copy(carry).wait_send()
    for k in (KB, 0, 1, 2):
        a_copy(1, k).start()
    pl.when(y == last)(b_onward)
    for k in range(KB):
        build_a(a_got.at[0, k], am_got.at[0], k)
        build_b(b_got.at[0], bm_got.at[0], k)
    multiply(False)

    b_copy(1, PARTS).wait_recv()
    b_copy(1, 0).wait_recv()
    for k in range(KB):
        b_copy(1, k + 1).wait_recv()
        build_b(b_got.at[1], bm_got.at[1], k)
    a_copy(1, KB).wait_recv()
    for k in range(KB):
        a_copy(1, k).wait_recv()
        build_a(a_got.at[1, k], am_got.at[1], k)
    multiply(False)

    def fill(slot, owner):
        for rank in range(CAPP):
            stage[slot * CAPP + rank] = prod[tbl_ref[owner * CAPP + rank]]

    def pair_at(ref, place):
        return ref.at[pl.ds(place * CAPP, CAPP)]

    def z_copy(d):
        dst = pair_at(out_ref, row) if d == 0 else pair_at(relay, d - 1)
        return send(pair_at(stage, SIDE + d), dst, z_s.at[d], z_r.at[d], across)

    def own_copy(d):
        return send(pair_at(stage, d), pair_at(out_ref, row), o_s.at[d], o_r.at[d], at_y(turned(d)))

    def onward_copy(d):
        return send(pair_at(relay, d - 1), pair_at(out_ref, other * SIDE + y),
                    w_s.at[d], w_r.at[d], at_y(turned(d)))

    order = (4, 3, 5, 2, 6, 1, 7, 0)
    def arrive(d):
        z_copy(d).wait_recv()
        if d == order[CHANGE]:
            @pl.when(early)
            def _():
                for peer in other_shift:
                    pl.semaphore_signal(turn, inc=1, device_id=peer, device_id_type=MESH)
        if d:
            onward_copy(d).start()

    def cross_pair(d):
        fill(SIDE + d, other * SIDE + turned(d))
        z_copy(d).start()

    def own_pairs():
        for d in range(1, SIDE):
            fill(d, half * SIDE + turned(d))
            own_copy(d).start()

    @pl.when(jnp.logical_not(early))
    def _():
        own_pairs()
        pl.semaphore_wait(turn, len(other_shift))

    for d in order[:WINDOW]:
        cross_pair(d)
    pl.when(early)(own_pairs)
    fill(0, row)
    kept = pltpu.make_async_copy(pair_at(stage, 0), pair_at(out_ref, row), l_s.at[0])
    kept.start()
    for n in range(WINDOW, SIDE):
        z_copy(order[n - WINDOW]).wait_send()
        cross_pair(order[n])
        if n >= LAG:
            arrive(order[n - LAG])
    for d in order[SIDE - LAG:]:
        arrive(d)

    for step in range(2):
        for k in range(KB + 1):
            a_copy(step, k).wait_send()

        @pl.when(y > 0)
        def _():
            for n in range(PARTS + 1):
                b_copy(step, n).wait_send()

    @pl.when(y < 2)
    def _():
        for n in range(1, PARTS):
            carry_copy(n).wait_send()
        cross_meta().wait_send()
        land_meta().wait_send()

    @pl.when(y < last)
    def _():
        land_copy().wait_send()
    kept.wait()
    for d in order[SIDE - WINDOW:]:
        z_copy(d).wait_send()
    for d in range(1, SIDE):
        own_copy(d).wait()
        onward_copy(d).wait()


def per_device(a_blocks, a_rowid, a_count, b_blocks, b_colid, b_count, dest_row):
    n_row = lax.axis_size("row")
    vmem = pl.BlockSpec(memory_space=pltpu.VMEM)
    f32, bf16 = jnp.float32, jnp.bfloat16
    smem = pl.BlockSpec(memory_space=pltpu.SMEM)
    dma = pltpu.SemaphoreType.DMA
    out = pl.pallas_call(
        kernel,
        out_shape=jax.ShapeDtypeStruct((n_row * CAPP, BS, BS), f32),
        in_specs=[vmem, smem, smem, vmem, smem, smem, smem],
        out_specs=pl.BlockSpec(memory_space=pl.ANY),
        scratch_shapes=[
            pltpu.VMEM((16, BS), jnp.int32),
            pltpu.VMEM((16, BS), jnp.int32),
            pltpu.SMEM((n_row * CAPP,), jnp.int32),
            pltpu.VMEM((2, KB, SLOTS * BS, BS), f32),
            pltpu.VMEM((2, KB * BS, SLOTS * BS), f32),
            pltpu.VMEM((2, 16, BS), jnp.int32),
            pltpu.VMEM((2, 16, BS), jnp.int32),
            pltpu.VMEM((PART, SLOTS * BS), f32),
            pltpu.VMEM((PART, SLOTS * BS), f32),
            pltpu.VMEM((16, BS), jnp.int32),
            pltpu.VMEM((RB * BS, KB * BS), bf16),
            pltpu.VMEM((RB * BS, KB * BS), bf16),
            pltpu.VMEM((KB * BS, CB * BS), bf16),
            pltpu.VMEM((KB * BS, CB * BS), bf16),
            pltpu.VMEM((BLOCKS + 1, BS, BS), f32),
            pltpu.VMEM((HALVES * SIDE * CAPP, BS, BS), f32),
            pltpu.VMEM(((SIDE - 1) * CAPP, BS, BS), f32),
            dma((2, KB + 1)), dma((2, KB + 1)), dma((2, PARTS + 1)), dma((2, PARTS + 1)),
            dma((PARTS,)), dma((1,)), dma((2,)), dma((2,)), dma((2,)),
            dma((SIDE,)), dma((SIDE,)), dma((SIDE,)), dma((SIDE,)),
            dma((SIDE,)), dma((SIDE,)), dma((1,)), pltpu.SemaphoreType.REGULAR,
        ],
        compiler_params=pltpu.CompilerParams(
            collective_id=0, has_side_effects=True, vmem_limit_bytes=48 * 2**20),
        cost_estimate=pl.CostEstimate(flops=2 * 3 * 3 * 512 * 384 * 768, bytes_accessed=4 * 2**20, transcendentals=0),
        name="panels",
    )(a_blocks[0], a_rowid, a_count, b_blocks.reshape(KB * BS, SLOTS * BS), b_colid, b_count, dest_row)
    return out[None]


def solution(mesh):
    placed = (
        P("row", "col", None, None),
        P("row", "col", None),
        P("row", "col"),
        P("row", "col", None, None),
        P("row", "col", None),
        P("row", "col"),
        P("row", "col", None),
    )
    return jax.shard_map(
        per_device,
        mesh=mesh,
        in_specs=placed,
        out_specs=P("row", "col", None, None),
        check_vma=False,
    )
```

```python
import jax
import jax.numpy as jnp
from jax import lax
from jax.experimental import pallas as pl
from jax.experimental.pallas import tpu as pltpu
from jax.sharding import PartitionSpec as P

MESH = pl.DeviceIdType.MESH
BS = 128
SLOTS = 3
RB = 4
CB = 6
KB = 3
CAPP = 2
LAG = 5
CHANGE = 5
WINDOW = 4
HALVES = 2
SIDE = 8
BLOCKS = RB * CB
PARTS = 4
PART = KB * BS // PARTS


def kernel(a_ref, a_id, a_used, b_ref, b_id, b_used, dest_ref, out_ref,
           am_ref, bm_ref, tbl_ref,
           a_got, b_got, am_got, bm_got, carry, crossed, crossed_m,
           pah, pal, pbh, pbl, prod, stage, relay,
           a_s, a_r, b_s, b_r, c_s, c_r, x_s, x_r, f_s,
           z_s, z_r, o_s, o_r, w_s, w_r, l_s, turn):
    row = lax.axis_index("row")
    col = lax.axis_index("col")
    n_col = lax.axis_size("col")
    half = row // SIDE
    y = lax.rem(row, SIDE)
    left = (row, lax.rem(col + n_col - 1, n_col))
    right = (row, lax.rem(col + 1, n_col))
    other = 1 - half
    across = (other * SIDE + y, col)
    inner = lax.rem(col // 2, SIDE)
    early = inner < SIDE // 2
    nearest = jnp.where(early, SIDE // 2, 2 * SIDE) - inner // 2 * 2

    def along_z(step):
        to = lax.rem(half * SIDE + inner + step, HALVES * SIDE)
        return (to // SIDE * SIDE + y, col + (lax.rem(to, SIDE) - inner) * 2)

    other_shift = [along_z(nearest + step) for step in (0, 2, SIDE, SIDE + 2)]

    first = (y == 0) | (y > PARTS)
    panel = jnp.where(first, 0, 1)
    part = jnp.where(first, lax.rem(SIDE - y, SIDE), y - 1)
    last = SIDE - 1

    def at_y(yy):
        return (half * SIDE + yy, col)

    def turned(d):
        return lax.rem(y + d, SIDE)

    def send(src, dst, ss, rs, to):
        return pltpu.make_async_remote_copy(
            src_ref=src, dst_ref=dst, send_sem=ss, recv_sem=rs, device_id=to, device_id_type=MESH)

    barrier = pltpu.get_barrier_semaphore()
    peers = [left, right, across] + other_shift + [at_y(turned(d)) for d in range(1, SIDE)]
    for peer in peers:
        pl.semaphore_signal(barrier, inc=1, device_id=peer, device_id_type=MESH)
    pl.semaphore_wait(barrier, len(peers))

    for k in range(KB):
        for t in range(SLOTS):
            a_mark = jnp.where(t < a_used[0, k], a_id[0, k, t], -1)
            b_mark = jnp.where(t < b_used[0, k], b_id[0, k, t], -1)
            am_ref[pl.ds(k * SLOTS + t, 1), :] = jnp.full((1, BS), a_mark, jnp.int32)
            bm_ref[pl.ds(k * SLOTS + t, 1), :] = jnp.full((1, BS), b_mark, jnp.int32)

    def a_copy(step, k):
        if k == KB:
            src = am_ref if step == 0 else am_got.at[0]
            return send(src, am_got.at[step], a_s.at[step, k], a_r.at[step, k], left)
        src = a_ref.at[k] if step == 0 else a_got.at[0, k]
        return send(src, a_got.at[step, k], a_s.at[step, k], a_r.at[step, k], left)

    up = at_y(lax.rem(y + SIDE - 1, SIDE))

    def rows_of(ref, n):
        return ref.at[pl.ds(pl.multiple_of(n * PART, PART), PART)]

    def b_copy(step, n):
        if n == PARTS:
            src = bm_ref if step == 0 else bm_got.at[0]
            return send(src, bm_got.at[step], b_s.at[step, n], b_r.at[step, n], up)
        src = b_ref if step == 0 else b_got.at[0]
        return send(rows_of(src, n), rows_of(b_got.at[step], n), b_s.at[step, n], b_r.at[step, n], up)

    def carry_copy(n):
        to = jnp.where(y == 0, SIDE - n, n + 1)
        return send(rows_of(b_ref, n), carry, c_s.at[n], c_r.at[0], at_y(to))

    def cross_copy(src):
        return send(src, crossed, x_s.at[0], x_r.at[0], across)

    def cross_last():
        return send(carry, rows_of(b_got.at[0], 1), x_s.at[0], b_r.at[0, 1], across)

    def cross_meta():
        return send(bm_ref, crossed_m, x_s.at[1], x_r.at[1], across)

    def land_copy():
        return send(crossed, rows_of(b_got.at[panel], part), f_s.at[0], b_r.at[panel, part], at_y(last))

    def land_meta():
        return send(crossed_m, bm_got.at[panel], f_s.at[1], b_r.at[panel, PARTS], at_y(last))

    @pl.when(y < 2)
    def _():
        cross_copy(rows_of(b_ref, 0)).start()
        cross_meta().start()
        for n in range(1, PARTS):
            carry_copy(n).start()

    @pl.when(y > 0)
    def _():
        for n in (PARTS, 0, 1, 2, 3):
            b_copy(0, n).start()

    for k in (KB, 0, 1, 2):
        a_copy(0, k).start()

    def build_a(src, meta, k):
        @pl.loop(0, RB)
        def _(i):
            total = jnp.zeros((BS, BS), jnp.float32)
            for t in range(SLOTS):
                total += jnp.where(meta[pl.ds(k * SLOTS + t, 1), :] == i, src[pl.ds(t * BS, BS), :], 0.0)
            high = total.astype(jnp.bfloat16)
            rows = pl.ds(pl.multiple_of(i * BS, BS), BS)
            pah[rows, pl.ds(k * BS, BS)] = high
            pal[rows, pl.ds(k * BS, BS)] = (total - high.astype(jnp.float32)).astype(jnp.bfloat16)

    def build_b(src, meta, k):
        @pl.loop(0, CB)
        def _(j):
            total = jnp.zeros((BS, BS), jnp.float32)
            for t in range(SLOTS):
                total += jnp.where(meta[pl.ds(k * SLOTS + t, 1), :] == j, src[pl.ds(k * BS, BS), pl.ds(t * BS, BS)], 0.0)
            high = total.astype(jnp.bfloat16)
            cols = pl.ds(pl.multiple_of(j * BS, BS), BS)
            pbh[pl.ds(k * BS, BS), cols] = high
            pbl[pl.ds(k * BS, BS), cols] = (total - high.astype(jnp.float32)).astype(jnp.bfloat16)

    def multiply(first):
        @pl.loop(0, CB // 2)
        def _(pair):
            cols = pl.ds(pl.multiple_of(pair * 2 * BS, 2 * BS), 2 * BS)
            bh = pbh[:, cols]
            bl = pbl[:, cols]
            for i in range(RB // 2):
                ah = pah[pl.ds(i * 2 * BS, 2 * BS), :]
                al = pal[pl.ds(i * 2 * BS, 2 * BS), :]
                part = (jnp.dot(ah, bl, preferred_element_type=jnp.float32)
                        + jnp.dot(al, bh, preferred_element_type=jnp.float32)
                        + jnp.dot(ah, bh, preferred_element_type=jnp.float32))
                for p in range(2):
                    for q in range(2):
                        block = (i * 2 + p) * CB + pair * 2 + q
                        piece = part[p * BS:(p + 1) * BS, q * BS:(q + 1) * BS]
                        prod[block] = piece if first else prod[block] + piece

    @pl.loop(0, HALVES * SIDE)
    def _(owner):
        first, second = BLOCKS, BLOCKS
        for m in range(BLOCKS - 1, -1, -1):
            hit = dest_ref[0, m, 0] == owner
            second = jnp.where(hit, first, second)
            first = jnp.where(hit, m, first)
        tbl_ref[owner * CAPP] = first
        tbl_ref[owner * CAPP + 1] = second

    for k in range(KB):
        build_a(a_ref.at[k], am_ref, k)
        build_b(b_ref, bm_ref, k)
    multiply(True)
    prod[BLOCKS] = jnp.zeros((BS, BS), jnp.float32)

    @pl.when((y > 1) & (y < last))
    def _():
        carry_copy(1).wait_recv()
        cross_copy(carry).start()

    @pl.when(y == last)
    def _():
        carry_copy(1).wait_recv()
        cross_last().start()

    def b_onward():
        for n in (PARTS, 0, 1, 2, 3):
            b_copy(0, n).wait_recv()

            @pl.when(y > 0)
            def _():
                b_copy(1, n).start()

    pl.when(y < last)(b_onward)
    for k in (KB, 0, 1, 2):
        a_copy(0, k).wait_recv()
        a_copy(1, k).start()

    @pl.when(y < 2)
    def _():
        cross_meta().wait_recv()
        land_meta().start()

    @pl.when(y < last)
    def _():
        cross_copy(carry).wait_recv()
        land_copy().start()

    cross_copy(carry).wait_send()
    pl.when(y == last)(b_onward)
    for k in range(KB):
        build_a(a_got.at[0, k], am_got.at[0], k)
        build_b(b_got.at[0], bm_got.at[0], k)
    multiply(False)

    b_copy(1, PARTS).wait_recv()
    b_copy(1, 0).wait_recv()
    for k in range(KB):
        b_copy(1, k + 1).wait_recv()
        build_b(b_got.at[1], bm_got.at[1], k)
    a_copy(1, KB).wait_recv()
    for k in range(KB):
        a_copy(1, k).wait_recv()
        build_a(a_got.at[1, k], am_got.at[1], k)
    multiply(False)

    def fill(slot, owner):
        for rank in range(CAPP):
            stage[slot * CAPP + rank] = prod[tbl_ref[owner * CAPP + rank]]

    def pair_at(ref, place):
        return ref.at[pl.ds(place * CAPP, CAPP)]

    def z_copy(d):
        dst = pair_at(out_ref, row) if d == 0 else pair_at(relay, d - 1)
        return send(pair_at(stage, SIDE + d), dst, z_s.at[d], z_r.at[d], across)

    def own_copy(d):
        return send(pair_at(stage, d), pair_at(out_ref, row), o_s.at[d], o_r.at[d], at_y(turned(d)))

    def onward_copy(d):
        return send(pair_at(relay, d - 1), pair_at(out_ref, other * SIDE + y),
                    w_s.at[d], w_r.at[d], at_y(turned(d)))

    order = (4, 3, 5, 2, 6, 1, 7, 0)
    def arrive(d):
        z_copy(d).wait_recv()
        if d == order[CHANGE]:
            @pl.when(early)
            def _():
                for peer in other_shift:
                    pl.semaphore_signal(turn, inc=1, device_id=peer, device_id_type=MESH)
        if d:
            onward_copy(d).start()

    def cross_pair(d):
        fill(SIDE + d, other * SIDE + turned(d))
        z_copy(d).start()

    def own_pairs():
        for d in range(1, SIDE):
            fill(d, half * SIDE + turned(d))
            own_copy(d).start()

    @pl.when(jnp.logical_not(early))
    def _():
        own_pairs()
        pl.semaphore_wait(turn, len(other_shift))

    for d in order[:WINDOW]:
        cross_pair(d)
    pl.when(early)(own_pairs)
    fill(0, row)
    kept = pltpu.make_async_copy(pair_at(stage, 0), pair_at(out_ref, row), l_s.at[0])
    kept.start()
    for n in range(WINDOW, SIDE):
        z_copy(order[n - WINDOW]).wait_send()
        cross_pair(order[n])
        if n >= LAG:
            arrive(order[n - LAG])
    for d in order[SIDE - LAG:]:
        arrive(d)

    for step in range(2):
        for k in range(KB + 1):
            a_copy(step, k).wait_send()

        @pl.when(y > 0)
        def _():
            for n in range(PARTS + 1):
                b_copy(step, n).wait_send()

    @pl.when(y < 2)
    def _():
        for n in range(1, PARTS):
            carry_copy(n).wait_send()
        cross_meta().wait_send()
        land_meta().wait_send()

    @pl.when(y < last)
    def _():
        land_copy().wait_send()
    kept.wait()
    for d in order[SIDE - WINDOW:]:
        z_copy(d).wait_send()
    for d in range(1, SIDE):
        own_copy(d).wait()
        onward_copy(d).wait()


def per_device(a_blocks, a_rowid, a_count, b_blocks, b_colid, b_count, dest_row):
    n_row = lax.axis_size("row")
    vmem = pl.BlockSpec(memory_space=pltpu.VMEM)
    f32, bf16 = jnp.float32, jnp.bfloat16
    smem = pl.BlockSpec(memory_space=pltpu.SMEM)
    dma = pltpu.SemaphoreType.DMA
    out = pl.pallas_call(
        kernel,
        out_shape=jax.ShapeDtypeStruct((n_row * CAPP, BS, BS), f32),
        in_specs=[vmem, smem, smem, vmem, smem, smem, smem],
        out_specs=pl.BlockSpec(memory_space=pl.ANY),
        scratch_shapes=[
            pltpu.VMEM((16, BS), jnp.int32),
            pltpu.VMEM((16, BS), jnp.int32),
            pltpu.SMEM((n_row * CAPP,), jnp.int32),
            pltpu.VMEM((2, KB, SLOTS * BS, BS), f32),
            pltpu.VMEM((2, KB * BS, SLOTS * BS), f32),
            pltpu.VMEM((2, 16, BS), jnp.int32),
            pltpu.VMEM((2, 16, BS), jnp.int32),
            pltpu.VMEM((PART, SLOTS * BS), f32),
            pltpu.VMEM((PART, SLOTS * BS), f32),
            pltpu.VMEM((16, BS), jnp.int32),
            pltpu.VMEM((RB * BS, KB * BS), bf16),
            pltpu.VMEM((RB * BS, KB * BS), bf16),
            pltpu.VMEM((KB * BS, CB * BS), bf16),
            pltpu.VMEM((KB * BS, CB * BS), bf16),
            pltpu.VMEM((BLOCKS + 1, BS, BS), f32),
            pltpu.VMEM((HALVES * SIDE * CAPP, BS, BS), f32),
            pltpu.VMEM(((SIDE - 1) * CAPP, BS, BS), f32),
            dma((2, KB + 1)), dma((2, KB + 1)), dma((2, PARTS + 1)), dma((2, PARTS + 1)),
            dma((PARTS,)), dma((1,)), dma((2,)), dma((2,)), dma((2,)),
            dma((SIDE,)), dma((SIDE,)), dma((SIDE,)), dma((SIDE,)),
            dma((SIDE,)), dma((SIDE,)), dma((1,)), pltpu.SemaphoreType.REGULAR,
        ],
        compiler_params=pltpu.CompilerParams(
            collective_id=0, has_side_effects=True, vmem_limit_bytes=48 * 2**20),
        cost_estimate=pl.CostEstimate(flops=2 * 3 * 3 * 512 * 384 * 768, bytes_accessed=4 * 2**20, transcendentals=0),
        name="panels",
    )(a_blocks[0], a_rowid, a_count, b_blocks.reshape(KB * BS, SLOTS * BS), b_colid, b_count, dest_row)
    return out[None]


def solution(mesh):
    placed = (
        P("row", "col", None, None),
        P("row", "col", None),
        P("row", "col"),
        P("row", "col", None, None),
        P("row", "col", None),
        P("row", "col"),
        P("row", "col", None),
    )
    return jax.shard_map(
        per_device,
        mesh=mesh,
        in_specs=placed,
        out_specs=P("row", "col", None, None),
        check_vma=False,
    )
```
